256 devices in a mesh: ctx: 128 (over x, z, y_hi, core), ch: 2 (over y_lo).
Axes of the slice: x: 4, y: 4 (y_hi: 2, y_lo: 2; y = y_hi * 2 + y_lo), z: 8, core: 2. Of those that a mesh axis runs over, the one named last changes fastest.
Arguments:
- queries: bfloat16 [32768, 4096], P('ctx', 'ch'), may hold values from -6 to 6
- keys: bfloat16 [32768, 4096], P('ctx', 'ch'), may hold values from -6 to 6
- values: bfloat16 [32768, 4096], P('ctx', 'ch'), may hold values from -6 to 6
- grad_out: bfloat16 [32768, 4096], P('ctx', 'ch'), may hold values from -0.0009765625 to 0.0009765625
Outputs:
- filter_grad: float32 [4, 1024], P('ch')
The draws below stay inside these ranges and needn't reach their ends.
All inputs are finite; a program needn't handle non-finite values.
Results may differ from the reference program's by a relative error of at most 0.004.
Values may be sent and summed in bfloat16 or wider, within the bound.
No kernel may reach another device: no remote copies, remote signals or barrier semaphores. Data moves between devices by JAX's collectives and lax.ppermute only.
A program may use at most 64 MiB of HBM per device.

```python
import jax
import jax.numpy as jnp
from jax import lax

D = 4096
GROUP_CH = 1024
GROUPS = 4
TOKENS = 32768
LAGS = 1024


def shard_levels(key, shape, pieces, low, largest):
    level, own = 1.0, jax.random.fold_in(key, 6)
    for dim, parts in pieces:
        draws = jnp.exp(jax.random.uniform(jax.random.fold_in(own, dim), (parts,), jnp.float32, low / len(pieces), largest / len(pieces)))
        level = level * jnp.repeat(draws, shape[dim] // parts).reshape([-1 if axis == dim else 1 for axis in range(len(shape))])
    return level


def normal_values(own_key, shape, width, limit, pieces=(), kind=jnp.bfloat16):
    result = width * jax.random.normal(own_key, shape, jnp.float32)
    if pieces:
        result = result * shard_levels(own_key, shape, pieces, -0.22, 0.18)
    return jnp.clip(result, -limit, limit).astype(kind)


def setup_inputs(seed: int = 0) -> dict:
    key_of = jax.random.split(jax.random.key(seed), 5)
    queries = normal_values(key_of[0], (TOKENS, D), 1.0, 6.0, ((0, 128), (1, 2)))
    keys = normal_values(key_of[1], (TOKENS, D), 1.0, 6.0, ((0, 128), (1, 2)))
    values = normal_values(key_of[2], (TOKENS, D), 1.0, 6.0, ((0, 128), (1, 2)))
    grad_out = normal_values(key_of[3], (TOKENS, D), (TOKENS * GROUP_CH) ** -0.5, 0.0009765625, ((0, 128), (1, 2)))
    return {"queries": queries, "keys": keys, "values": values, "grad_out": grad_out}


def reference(queries, keys, values, grad_out):
    mixed = (keys.astype(jnp.float32) * values.astype(jnp.float32)).astype(jnp.bfloat16)
    weighted = (queries.astype(jnp.float32) * grad_out.astype(jnp.float32)).astype(jnp.bfloat16)
    length = 2 * TOKENS
    part_cols = min(GROUP_CH, 64)
    spectrum = length // 2 + 1

    def per_group(group_index):
        def add_piece(totals, piece_index):
            start = (group_index * GROUP_CH + piece_index * part_cols).astype(jnp.int32)
            source = lax.dynamic_slice_in_dim(mixed, start, part_cols, 1).astype(jnp.float32)
            target = lax.dynamic_slice_in_dim(weighted, start, part_cols, 1).astype(jnp.float32)
            source_freq = jnp.fft.rfft(source, n=length, axis=0)
            target_freq = jnp.fft.rfft(target, n=length, axis=0)
            joined = jnp.sum(jnp.conj(source_freq) * target_freq, axis=1)
            return (totals[0] + joined.real, totals[1] + joined.imag), None

        zeros_pair = (jnp.zeros(spectrum, jnp.float32), jnp.zeros(spectrum, jnp.float32))
        summed, ignored = lax.scan(add_piece, zeros_pair, jnp.arange(GROUP_CH // part_cols, dtype=jnp.int32))
        series = jnp.fft.irfft(summed[0] + 1j * summed[1], n=length)
        return series[:LAGS].astype(jnp.float32)

    return lax.map(per_group, jnp.arange(GROUPS, dtype=jnp.int32))
```

```python
import jax
import jax.numpy as jnp
from jax import lax
from jax.experimental import pallas as pl
from jax.experimental.pallas import tpu as pltpu
from jax.sharding import PartitionSpec as P

BLK = 256
CH = 512
HALF = 256
LAGS = 1024
MIB = 1024 * 1024
NT = (((1,), (1,)), ((), ()))


def products(q, k, v, g):
    weighted = (q.astype(jnp.float32) * g.astype(jnp.float32)).astype(jnp.bfloat16)
    mixed = (k.astype(jnp.float32) * v.astype(jnp.float32)).astype(jnp.bfloat16)
    return weighted, mixed


def deal_kernel(me, q, k, v, g, near1, near2, far1, far2, flip, own):
    step = pl.program_id(0)
    weighted, mixed = products(q[...], k[...], v[...], g[...])

    def split(first, second):
        first[0] = mixed[:, :HALF]
        first[1] = weighted[:, HALF:]
        second[0] = mixed[:, HALF:]
        second[1] = weighted[:, :HALF]

    def whole(out):
        out[0] = weighted
        out[1] = mixed

    pl.when(step == 0)(lambda: split(near1, near2))
    pl.when(step == 1)(lambda: split(far1, far2))
    pl.when(step == 2)(lambda: whole(flip))
    pl.when(step == 3)(lambda: whole(own))


def deal(me, queries, keys, values, grad_out):
    def block(step, me):
        other_y = 1 - step // 2
        other_core = step % 2 - (step // 2) * (2 * (step % 2) - 1)
        return 0, (me[1] ^ other_core) * 2 + (me[0] ^ other_y)

    piece = pl.BlockSpec((BLK, CH), block)
    half = pl.BlockSpec((2, BLK, HALF), lambda step, me: (0, 0, 0))
    full = pl.BlockSpec((2, BLK, CH), lambda step, me: (0, 0, 0))
    half_t = jax.ShapeDtypeStruct((2, BLK, HALF), jnp.bfloat16)
    full_t = jax.ShapeDtypeStruct((2, BLK, CH), jnp.bfloat16)
    return pl.pallas_call(
        deal_kernel,
        grid_spec=pltpu.PrefetchScalarGridSpec(
            num_scalar_prefetch=1,
            grid=(4,),
            in_specs=[piece] * 4,
            out_specs=[half] * 4 + [full] * 2,
        ),
        out_shape=[half_t] * 4 + [full_t] * 2,
        compiler_params=pltpu.CompilerParams(vmem_limit_bytes=24 * MIB),
        name="deal",
    )(me, queries, keys, values, grad_out)


def lag_sums(table):
    wide = 5 * BLK
    rows = BLK
    while rows > 1:
        half = rows // 2
        low, high = table[:half], table[half:rows]
        if half % 128 == 0:
            wide = wide - half
            table = low[:, :wide] + high[:, half : half + wide]
        else:
            table = low + pltpu.roll(high, wide - half, 1)
        rows = half
    return table


def correlate_kernel(
    me, own, flip, near1, near2, far1, far2, mix_e, mix_l, wei_e, wei_l, out,
    mix_a, wei_a, mix_b, wei_b, table, sems,
):
    here = 2 * me[0]
    there = 2 - here
    spots = (here + me[1], here + 1 - me[1], there + me[1], there + 1 - me[1])
    copies = []

    def bring(src, dst, spot):
        at = pl.ds(pl.multiple_of(spot * BLK, BLK), HALF)
        copy = pltpu.make_async_copy(src, dst.at[:, at], sems.at[len(copies)])
        copy.start()
        copies.append(copy)

    for ref, spot in ((own, spots[0]), (flip, spots[1])):
        bring(ref.at[0, :, pl.ds(0, HALF)], wei_a, spot)
        bring(ref.at[0, :, pl.ds(HALF, HALF)], wei_b, spot)
        bring(ref.at[1, :, pl.ds(0, HALF)], mix_a, 4 + spot)
        bring(ref.at[1, :, pl.ds(HALF, HALF)], mix_b, spot)
    for first, second, spot in ((near1, near2, spots[2]), (far1, far2, spots[3])):
        bring(first.at[0], mix_a, 4 + spot)
        bring(first.at[1], wei_b, spot)
        bring(second.at[0], mix_b, spot)
        bring(second.at[1], wei_a, spot)
    for part, (mix, wei) in enumerate(((mix_e, wei_e), (mix_l, wei_l))):
        for i in range(2):
            bring(mix.at[i], mix_a, spots[2 * part + i])
            bring(wei.at[i], wei_b, 4 + spots[2 * part + i])
    for copy in copies:
        copy.wait()
    for d in range(5):
        one = lax.dot_general(
            mix_a[:, pl.ds((4 - d) * BLK, 4 * BLK)], wei_a[...], NT,
            preferred_element_type=jnp.float32,
        )
        two = lax.dot_general(
            mix_b[...], wei_b[:, pl.ds(d * BLK, 4 * BLK)], NT,
            preferred_element_type=jnp.float32,
        )
        table[:, pl.ds(d * BLK, BLK)] = one + two
    sums = lag_sums(table[...])
    for i in range(8):
        out[i : i + 1, :] = sums[:, i * 128 : (i + 1) * 128]


def correlate(me, *arrays):
    anywhere = pl.BlockSpec(memory_space=pl.ANY)
    return pl.pallas_call(
        correlate_kernel,
        in_specs=[pl.BlockSpec(memory_space=pltpu.SMEM)] + [anywhere] * len(arrays),
        out_specs=pl.BlockSpec(memory_space=pltpu.VMEM),
        out_shape=jax.ShapeDtypeStruct((8, 128), jnp.float32),
        scratch_shapes=[
            pltpu.VMEM((BLK, 8 * BLK), jnp.bfloat16),
            pltpu.VMEM((BLK, 4 * BLK), jnp.bfloat16),
            pltpu.VMEM((BLK, 4 * BLK), jnp.bfloat16),
            pltpu.VMEM((BLK, 8 * BLK), jnp.bfloat16),
            pltpu.VMEM((BLK, 5 * BLK), jnp.float32),
            pltpu.SemaphoreType.DMA((24,)),
        ],
        compiler_params=pltpu.CompilerParams(vmem_limit_bytes=24 * MIB),
        name="correlate",
    )(me, *arrays)


def swap(value, quads, far, flip):
    pairs = [
        ((q * 2 + y) * 2 + c, (q * 2 + (y ^ far)) * 2 + (c ^ flip))
        for q in range(quads) for y in range(2) for c in range(2)
    ]
    return lax.ppermute(value, "ctx", pairs)


def shift(value, quads, by):
    pairs = [
        (q * 4 + e, (q + by) * 4 + e)
        for q in range(quads) for e in range(4) if 0 <= q + by < quads
    ]
    return lax.ppermute(value, "ctx", pairs)


def on_device(queries, keys, values, grad_out):
    quads = lax.axis_size("ctx") // 4
    place = lax.axis_index("ctx")
    me = jnp.stack([(place // 2) % 2, place % 2]).astype(jnp.int32)
    near1, near2, far1, far2, flip, own = deal(me, queries, keys, values, grad_out)
    flip = swap(flip, quads, 0, 1)
    near1 = swap(near1, quads, 1, 0)
    far1 = swap(far1, quads, 1, 1)
    near2 = swap(near2, quads, 1, 0)
    far2 = swap(far2, quads, 1, 1)
    mix_e = shift(jnp.stack([own[1, :, :HALF], flip[1, :, :HALF]]), quads, 1)
    wei_e = shift(jnp.stack([own[0, :, HALF:], flip[0, :, HALF:]]), quads, -1)
    mix_l = shift(jnp.stack([near1[0], far1[0]]), quads, 1)
    wei_l = shift(jnp.stack([near1[1], far1[1]]), quads, -1)
    part = correlate(
        me, own, flip, near1, near2, far1, far2, mix_e, mix_l, wei_e, wei_l
    )
    part = part + swap(part, quads, 1, 0)
    groups = [[q * 4 + e for q in range(quads)] for e in range(4)]
    spread = jnp.broadcast_to(part[None], (quads, 8, 128))
    gathered = lax.all_to_all(spread, "ctx", 0, 0, axis_index_groups=groups)
    mine = jnp.sum(gathered, axis=0).reshape(1, LAGS)
    other = swap(mine, quads, 0, 1)
    first = place % 2 == 0
    return jnp.concatenate(
        [jnp.where(first, mine, other), jnp.where(first, other, mine)], axis=0
    )


def solution(mesh):
    spec = P("ctx", "ch")
    return jax.shard_map(
        on_device, mesh=mesh, in_specs=(spec,) * 4, out_specs=P("ch", None), check_vma=False
    )
```

```python
import jax
import jax.numpy as jnp
from jax import lax
from jax.experimental import pallas as pl
from jax.experimental.pallas import tpu as pltpu
from jax.sharding import PartitionSpec as P

BLK = 256
CH = 512
LAGS = 1024
MIB = 1024 * 1024
DEAL_MIB = 56
NT = (((1,), (1,)), ((), ()))
BF16 = jnp.bfloat16


def columns(yh, core):
    return pl.ds(pl.multiple_of(yh * 2 * CH + core * CH, CH), CH)


def product(a, b):
    return (a.astype(jnp.float32) * b.astype(jnp.float32)).astype(BF16)


def fetch(core, slots, sems, arrays, wanted):
    queries, keys, values, grad_out = arrays
    mixed, weighted = (keys, values), (queries, grad_out)

    def start(here):
        for i, (same, moving, cols) in enumerate(wanted):
            target = here if same else 1 - here
            pair = mixed if (target == 0) == moving else weighted
            for j in range(2):
                pltpu.make_async_copy(
                    pair[j].at[:, cols], slots.at[2 * i + j], sems.at[2 * i + j]
                ).start()

    pl.when(core == 0)(lambda: start(0))
    pl.when(core == 1)(lambda: start(1))

    def get(i):
        for j in range(2):
            pltpu.make_async_copy(
                keys.at[:, wanted[i][2]], slots.at[2 * i + j], sems.at[2 * i + j]
            ).wait()
        return product(slots[2 * i], slots[2 * i + 1])

    return get


def position():
    place = lax.axis_index("ctx")
    return (place // 2) % 2, place % 2


def deal_first(q, k, v, g, keep, give, slots, sems):
    yh, core = position()
    wanted = (
        (False, True, columns(1 - yh, 1 - core)),
        (False, True, columns(yh, 1 - core)),
        (True, True, columns(1 - yh, core)),
    )
    get = fetch(core, slots, sems, (q, k, v, g), wanted)
    give[0] = get(0)
    give[1] = get(1)
    keep[...] = get(2)


def deal_second(q, k, v, g, moving, keep, give, fixed, slots, sems):
    yh, core = position()
    wanted = (
        (False, False, columns(1 - yh, 1 - core)),
        (False, False, columns(yh, 1 - core)),
        (True, False, columns(1 - yh, core)),
        (True, True, columns(yh, core)),
        (True, False, columns(yh, core)),
    )
    get = fetch(core, slots, sems, (q, k, v, g), wanted)
    give[0] = get(0)
    give[1] = get(1)
    keep[...] = get(2)
    moving[...] = get(3)
    fixed[...] = get(4)


def deal(body, name, outs, pieces, arrays):
    vmem = pl.BlockSpec(memory_space=pltpu.VMEM)
    return pl.pallas_call(
        body,
        in_specs=[pl.BlockSpec(memory_space=pl.ANY)] * 4,
        out_specs=[vmem] * len(outs),
        out_shape=[pltpu.VMEM(shape, BF16) for shape in outs],
        scratch_shapes=[
            pltpu.VMEM((2 * pieces, BLK, CH), BF16),
            pltpu.SemaphoreType.DMA((2 * pieces,)),
        ],
        compiler_params=pltpu.CompilerParams(vmem_limit_bytes=DEAL_MIB * MIB),
        name=name,
    )(*arrays)


def gather_kernel(beyond, near, far, onto, moving):
    onto[...] = far[...]
    moving[0:2] = beyond[...]
    moving[4:6] = near[...]
    moving[6:8] = far[...]


def gather(beyond, near, far):
    vmem = pl.BlockSpec(memory_space=pltpu.VMEM)
    return pl.pallas_call(
        gather_kernel,
        in_specs=[vmem] * 3,
        out_specs=[vmem] * 2,
        out_shape=[
            jax.ShapeDtypeStruct((2, BLK, CH), BF16),
            jax.ShapeDtypeStruct((8, BLK, CH), BF16),
        ],
        compiler_params=pltpu.CompilerParams(vmem_limit_bytes=40 * MIB),
        name="gather",
    )(beyond, near, far)


def lag_sums(table):
    wide = 5 * BLK
    rows = BLK
    while rows > 1:
        half = rows // 2
        low, high = table[:half], table[half:rows]
        if half % 128 == 0:
            wide = wide - half
            table = low[:, :wide] + high[:, half : half + wide]
        else:
            table = low + pltpu.roll(high, wide - half, 1)
        rows = half
    return table


def correlate_kernel(moving_in, onto, own, flip, far, out, moving, table):
    yh, core = position()
    home = 2 * yh + core
    moving[2:4] = onto[...]

    def fill(here):
        for d in range(5):
            total = None
            for i, fixed in enumerate((own, flip.at[1], far.at[0], far.at[1])):
                if here == 0:
                    at = 4 + (home ^ i) - d
                    there = jnp.where(at >= 4, 4, 0) + ((at & 3) ^ home)
                    pair = moving[there], fixed[...]
                else:
                    at = (home ^ i) + d
                    there = jnp.where(at < 4, 4, 0) + ((at & 3) ^ home)
                    pair = fixed[...], moving[there]
                dot = lax.dot_general(*pair, NT, preferred_element_type=jnp.float32)
                total = dot if total is None else total + dot
            table[:, pl.ds(d * BLK, BLK)] = total

    pl.when(core == 0)(lambda: fill(0))
    pl.when(core == 1)(lambda: fill(1))
    sums = lag_sums(table[...])
    for i in range(8):
        out[i : i + 1, :] = sums[:, i * 128 : (i + 1) * 128]


def correlate(moving, *arrays):
    vmem = pl.BlockSpec(memory_space=pltpu.VMEM)
    return pl.pallas_call(
        correlate_kernel,
        in_specs=[vmem] * (1 + len(arrays)),
        out_specs=[vmem, vmem],
        out_shape=[
            jax.ShapeDtypeStruct((8, 128), jnp.float32),
            jax.ShapeDtypeStruct(moving.shape, BF16),
        ],
        input_output_aliases={0: 1},
        scratch_shapes=[pltpu.VMEM((BLK, 5 * BLK), jnp.float32)],
        compiler_params=pltpu.CompilerParams(vmem_limit_bytes=40 * MIB),
        name="correlate",
    )(moving, *arrays)[0]


def swap(value, quads, far, flip):
    pairs = [
        ((q * 2 + y) * 2 + c, (q * 2 + (y ^ far)) * 2 + (c ^ flip))
        for q in range(quads) for y in range(2) for c in range(2)
    ]
    return lax.ppermute(value, "ctx", pairs)


def onward(value, quads):
    pairs = [
        (q * 4 + e, (q + 1 - 2 * (e % 2)) * 4 + e)
        for q in range(quads) for e in range(4) if 0 <= q + 1 - 2 * (e % 2) < quads
    ]
    return lax.ppermute(value, "ctx", pairs)


def on_device(queries, keys, values, grad_out):
    quads = lax.axis_size("ctx") // 4
    arrays = (queries, keys, values, grad_out)
    one, two = (BLK, CH), (2, BLK, CH)
    keep, give = deal(deal_first, "deal_first", [one, two], 3, arrays)
    got = swap(give, quads, 0, 1)
    far_moving = swap(jnp.stack([keep, got[0]]), quads, 1, 0)
    moving, keep, give, fixed = deal(
        deal_second, "deal_second", [one, one, two, one], 5, arrays
    )
    near_moving = jnp.stack([moving, got[1]])
    got = swap(give, quads, 0, 1)
    far_fixed = swap(jnp.stack([keep, got[0]]), quads, 1, 0)
    beyond = onward(near_moving, quads)
    onto, table = gather(beyond, near_moving, far_moving)
    onto = onward(onto, quads)
    part = correlate(table, onto, fixed, got, far_fixed)
    part = part + swap(part, quads, 0, 1)
    groups = [[q * 4 + y * 2 + c for q in range(quads) for y in range(2)] for c in range(2)]
    spread = jnp.broadcast_to(part[None], (2 * quads, 8, 128))
    gathered = lax.all_to_all(spread, "ctx", 0, 0, axis_index_groups=groups)
    return jnp.sum(gathered.reshape(quads, 2, 8, 128), axis=0).reshape(2, LAGS)


def solution(mesh):
    spec = P("ctx", "ch")
    return jax.shard_map(
        on_device, mesh=mesh, in_specs=(spec,) * 4, out_specs=P("ch", None), check_vma=False
    )
```

```python
import jax
import jax.numpy as jnp
from jax import lax
from jax.experimental import pallas as pl
from jax.experimental.pallas import tpu as pltpu
from jax.sharding import PartitionSpec as P

BLK = 256
CH = 512
LAGS = 1024
MIB = 1024 * 1024
DEAL_MIB = 56
MAIN_COST = 4 * 10**9
NT = (((1,), (1,)), ((), ()))
BF16 = jnp.bfloat16


def columns(yh, core):
    return pl.ds(pl.multiple_of(yh * 2 * CH + core * CH, CH), CH)


def product(a, b):
    return (a.astype(jnp.float32) * b.astype(jnp.float32)).astype(BF16)


def fetch(core, slots, sems, arrays, wanted):
    queries, keys, values, grad_out = arrays
    mixed, weighted = (keys, values), (queries, grad_out)

    def start(here):
        for i, (same, moving, cols) in enumerate(wanted):
            target = here if same else 1 - here
            pair = mixed if (target == 0) == moving else weighted
            for j in range(2):
                pltpu.make_async_copy(
                    pair[j].at[:, cols], slots.at[2 * i + j], sems.at[2 * i + j]
                ).start()

    pl.when(core == 0)(lambda: start(0))
    pl.when(core == 1)(lambda: start(1))

    def get(i):
        for j in range(2):
            pltpu.make_async_copy(
                keys.at[:, wanted[i][2]], slots.at[2 * i + j], sems.at[2 * i + j]
            ).wait()
        return product(slots[2 * i], slots[2 * i + 1])

    return get


def position():
    place = lax.axis_index("ctx")
    return (place // 2) % 2, place % 2


def deal_first(q, k, v, g, far, give, own, slots, sems):
    yh, core = position()
    wanted = (
        (False, True, columns(yh, 1 - core)),
        (True, True, columns(1 - yh, core)),
        (False, True, columns(1 - yh, 1 - core)),
        (True, True, columns(yh, core)),
    )
    get = fetch(core, slots, sems, (q, k, v, g), wanted)
    give[...] = get(0)
    far[0] = get(1)
    far[1] = get(2)
    own[...] = get(3)


def deal_second(q, k, v, g, give, give_own, keep, own, slots, sems):
    yh, core = position()
    wanted = (
        (False, False, columns(1 - yh, 1 - core)),
        (False, False, columns(yh, 1 - core)),
        (True, False, columns(1 - yh, core)),
        (True, False, columns(yh, core)),
    )
    get = fetch(core, slots, sems, (q, k, v, g), wanted)
    give[...] = get(0)
    give_own[...] = get(1)
    keep[...] = get(2)
    own[...] = get(3)


def deal(body, name, shapes, arrays):
    vmem = pl.BlockSpec(memory_space=pltpu.VMEM)
    return pl.pallas_call(
        body,
        in_specs=[pl.BlockSpec(memory_space=pl.ANY)] * 4,
        out_specs=[vmem] * len(shapes),
        out_shape=[pltpu.VMEM(shape, BF16) for shape in shapes],
        scratch_shapes=[
            pltpu.VMEM((8, BLK, CH), BF16),
            pltpu.SemaphoreType.DMA((8,)),
        ],
        compiler_params=pltpu.CompilerParams(vmem_limit_bytes=DEAL_MIB * MIB),
        name=name,
    )(*arrays)


def gather_kernel(beyond, near, far, onto, pass_on, moving, give):
    give[0] = pass_on[...]
    give[1] = far[1]
    moving[0:2] = beyond[...]
    moving[2] = onto[...]
    moving[3] = jnp.zeros((BLK, CH), BF16)
    moving[4:6] = near[...]
    moving[6] = far[0]
    moving[7] = jnp.zeros((BLK, CH), BF16)


def gather(*arrays):
    vmem = pl.BlockSpec(memory_space=pltpu.VMEM)
    return pl.pallas_call(
        gather_kernel,
        in_specs=[vmem] * 5,
        out_specs=[vmem] * 2,
        out_shape=[
            jax.ShapeDtypeStruct((8, BLK, CH), BF16),
            jax.ShapeDtypeStruct((2, BLK, CH), BF16),
        ],
        compiler_params=pltpu.CompilerParams(vmem_limit_bytes=40 * MIB),
        name="gather",
    )(*arrays)


def lag_sums(table):
    wide = 5 * BLK
    rows = BLK
    while rows > 1:
        half = rows // 2
        low, high = table[:half], table[half:rows]
        if half % 128 == 0:
            wide = wide - half
            table = low[:, :wide] + high[:, half : half + wide]
        else:
            table = low + pltpu.roll(high, wide - half, 1)
        rows = half
    return table


def block_dot(core, moving, fixed):
    pair = (moving, fixed) if core == 0 else (fixed, moving)
    return lax.dot_general(*pair, NT, preferred_element_type=jnp.float32)


def on_core(core, body):
    pl.when(core == 0)(lambda: body(0))
    pl.when(core == 1)(lambda: body(1))


def main_kernel(moving, own, flip, far, table):
    yh, core = position()
    home = 2 * yh + core

    def body(here):
        for d in range(5):
            total = None
            for i, fixed in enumerate((own, flip, far.at[0], far.at[1])):
                if here == 0:
                    at = 4 + (home ^ i) - d
                    there = jnp.where(at >= 4, 4, 0) + ((at & 3) ^ home)
                else:
                    at = (home ^ i) + d
                    there = jnp.where(at < 4, 4, 0) + ((at & 3) ^ home)
                dot = block_dot(here, moving[there], fixed[...])
                total = dot if total is None else total + dot
            table[:, pl.ds(d * BLK, BLK)] = total

    on_core(core, body)


def tail_kernel(table_in, last, own, flip, far, out, table):
    yh, core = position()
    home = 2 * yh + core

    def body(here):
        def add(d, which, fixed):
            at = pl.ds(pl.multiple_of(d * BLK, BLK), BLK)
            table[:, at] = table_in[:, at] + block_dot(here, last[which], fixed[...])

        for i, fixed in enumerate((own, flip, far.at[0])):
            gap = (home ^ i) - (home ^ 3)
            gap = gap if here == 0 else -gap
            add(gap & 3, (gap > 0).astype(jnp.int32), fixed)
        add(0, 1, far.at[1])
        add(4, 0, far.at[1])

    on_core(core, body)
    sums = lag_sums(table[...])
    for i in range(8):
        out[i : i + 1, :] = sums[:, i * 128 : (i + 1) * 128]


def correlate(moving, last, *fixed):
    vmem = pl.BlockSpec(memory_space=pltpu.VMEM)
    params = pltpu.CompilerParams(vmem_limit_bytes=40 * MIB)
    table_t = jax.ShapeDtypeStruct((BLK, 5 * BLK), jnp.float32)
    table = pl.pallas_call(
        main_kernel,
        in_specs=[vmem] * 4,
        out_specs=vmem,
        out_shape=table_t,
        compiler_params=params,
        cost_estimate=pl.CostEstimate(
            flops=MAIN_COST, bytes_accessed=4 * MIB, transcendentals=0
        ),
        name="main",
    )(moving, *fixed)
    return pl.pallas_call(
        tail_kernel,
        in_specs=[vmem] * 5,
        out_specs=vmem,
        out_shape=jax.ShapeDtypeStruct((8, 128), jnp.float32),
        scratch_shapes=[pltpu.VMEM((BLK, 5 * BLK), jnp.float32)],
        compiler_params=params,
        name="tail",
    )(table, last, *fixed)


def swap(value, quads, far, flip):
    pairs = [
        ((q * 2 + y) * 2 + c, (q * 2 + (y ^ far)) * 2 + (c ^ flip))
        for q in range(quads) for y in range(2) for c in range(2)
    ]
    return lax.ppermute(value, "ctx", pairs)


def onward(value, quads, first=1):
    pairs = []
    for q in range(quads):
        for e in range(4):
            to = q + first * (1 - 2 * (e % 2))
            if 0 <= to < quads:
                pairs.append((q * 4 + e, to * 4 + e))
    return lax.ppermute(value, "ctx", pairs)


def on_device(queries, keys, values, grad_out):
    quads = lax.axis_size("ctx") // 4
    arrays = (queries, keys, values, grad_out)
    one, two = (BLK, CH), (2, BLK, CH)
    far_moving, give, own_moving = deal(deal_first, "deal_first", [two, one, one], arrays)
    flip_moving = swap(give, quads, 0, 1)
    far_moving = swap(far_moving, quads, 1, 0)
    near_moving = jnp.stack([own_moving, flip_moving])
    beyond = onward(near_moving, quads)
    give, give_own, keep, own_fixed = deal(deal_second, "deal_second", [one] * 4, arrays)
    far_fixed = swap(jnp.stack([keep, swap(give, quads, 0, 1)]), quads, 1, 0)
    flip_fixed = swap(give_own, quads, 0, 1)
    onto_far = onward(far_moving[1], quads, -1)
    onto_near = onward(far_moving[0], quads)
    moving, give = gather(beyond, near_moving, far_moving, onto_near, onto_far)
    last = swap(give, quads, 0, 1)
    part = correlate(moving, last, own_fixed, flip_fixed, far_fixed)
    part = part + swap(part, quads, 0, 1)
    groups = [[q * 4 + y * 2 + c for q in range(quads) for y in range(2)] for c in range(2)]
    spread = jnp.broadcast_to(part[None], (2 * quads, 8, 128))
    gathered = lax.all_to_all(spread, "ctx", 0, 0, axis_index_groups=groups)
    return jnp.sum(gathered.reshape(quads, 2, 8, 128), axis=0).reshape(2, LAGS)


def solution(mesh):
    spec = P("ctx", "ch")
    return jax.shard_map(
        on_device, mesh=mesh, in_specs=(spec,) * 4, out_specs=P("ch", None), check_vma=False
    )
```

```python
import functools

import jax
import jax.numpy as jnp
from jax import lax
from jax.experimental import pallas as pl
from jax.experimental.pallas import tpu as pltpu
from jax.sharding import PartitionSpec as P

BLK = 256
CH = 512
LAGS = 1024
MIB = 1024 * 1024
DEAL_MIB = 56
MAIN_COST = 15 * 2 * BLK * BLK * CH
NT = (((1,), (1,)), ((), ()))
BF16 = jnp.bfloat16


def columns(yh, core):
    return pl.ds(pl.multiple_of(yh * 2 * CH + core * CH, CH), CH)


def product(a, b):
    return (a.astype(jnp.float32) * b.astype(jnp.float32)).astype(BF16)


def fetch(core, slots, sems, arrays, wanted):
    queries, keys, values, grad_out = arrays
    mixed, weighted = (keys, values), (queries, grad_out)

    def start(here):
        for i, (same, moving, cols) in enumerate(wanted):
            target = here if same else 1 - here
            pair = mixed if (target == 0) == moving else weighted
            for j in range(2):
                pltpu.make_async_copy(
                    pair[j].at[:, cols], slots.at[2 * i + j], sems.at[2 * i + j]
                ).start()

    pl.when(core == 0)(lambda: start(0))
    pl.when(core == 1)(lambda: start(1))

    def get(i):
        for j in range(2):
            pltpu.make_async_copy(
                keys.at[:, wanted[i][2]], slots.at[2 * i + j], sems.at[2 * i + j]
            ).wait()
        return product(slots[2 * i], slots[2 * i + 1])

    return get


def position():
    place = lax.axis_index("ctx")
    return (place // 2) % 2, place % 2


def deal_first(q, k, v, g, far, give, own, slots, sems):
    yh, core = position()
    wanted = (
        (False, True, columns(yh, 1 - core)),
        (True, True, columns(1 - yh, core)),
        (False, True, columns(1 - yh, 1 - core)),
        (True, True, columns(yh, core)),
    )
    get = fetch(core, slots, sems, (q, k, v, g), wanted)
    give[...] = get(0)
    far[0] = get(1)
    far[1] = get(2)
    own[...] = get(3)


def deal_second(q, k, v, g, top, low, give_own, keep, own, slots, sems):
    yh, core = position()
    wanted = (
        (False, False, columns(1 - yh, 1 - core)),
        (False, False, columns(yh, 1 - core)),
        (True, False, columns(1 - yh, core)),
        (True, False, columns(yh, core)),
    )
    get = fetch(core, slots, sems, (q, k, v, g), wanted)
    give = get(0)
    top[...] = give[: BLK // 2]
    low[...] = give[BLK // 2 :]
    give_own[...] = get(1)
    keep[...] = get(2)
    own[...] = get(3)


def deal(body, name, shapes, arrays):
    vmem = pl.BlockSpec(memory_space=pltpu.VMEM)
    return pl.pallas_call(
        body,
        in_specs=[pl.BlockSpec(memory_space=pl.ANY)] * 4,
        out_specs=[vmem] * len(shapes),
        out_shape=[pltpu.VMEM(shape, BF16) for shape in shapes],
        scratch_shapes=[
            pltpu.VMEM((8, BLK, CH), BF16),
            pltpu.SemaphoreType.DMA((8,)),
        ],
        compiler_params=pltpu.CompilerParams(vmem_limit_bytes=DEAL_MIB * MIB),
        name=name,
    )(*arrays)


def lag_sums(table):
    wide = 5 * BLK - 128
    table = table[:128, :wide] + table[128:, 128:]
    total = table[:8]
    for row in range(8, 128, 8):
        total = total + pltpu.roll(table[row : row + 8], wide - row, 1)
    sums = total[:1]
    for row in range(1, 8):
        sums = sums + pltpu.roll(total[row : row + 1], wide - row, 1)
    return sums


def block_dot(core, moving, fixed):
    pair = (moving, fixed) if core == 0 else (fixed, moving)
    return lax.dot_general(*pair, NT, preferred_element_type=jnp.float32)


def by_home(body):
    place = lax.rem(lax.axis_index("ctx"), 4)
    for home in range(4):
        pl.when(place == home)(functools.partial(body, home))


def columns_of(d):
    return pl.ds(d * BLK, BLK)


def main_kernel(beyond, near, far, last, onto, own, flip, fixed, table):
    def body(home):
        core = home & 1
        here = {home: near.at[0], home ^ 1: near.at[1], home ^ 2: far.at[0], home ^ 3: last}
        there = {home: beyond.at[0], home ^ 1: beyond.at[1], home ^ 2: onto}
        stay = {home: own, home ^ 1: flip, home ^ 2: fixed.at[0], home ^ 3: fixed.at[1]}
        for d in range(5):
            total = None
            for block, ref in stay.items():
                other = block - d if core == 0 else block + d
                source = here if 0 <= other < 4 else there
                if (other & 3) in source:
                    dot = block_dot(core, source[other & 3][...], ref[...])
                    total = dot if total is None else total + dot
            table[:, columns_of(d)] = total

    by_home(body)


def tail_kernel(table_in, onto, own, flip, fixed, out, table):
    def body(home):
        core = home & 1
        stay = {home: own, home ^ 1: flip, home ^ 2: fixed.at[0], home ^ 3: fixed.at[1]}
        for d in range(5):
            block = (home ^ 3) + (d - 4 if core == 0 else 4 - d)
            total = table_in[:, columns_of(d)]
            if 0 <= block < 4:
                total = total + block_dot(core, onto[...], stay[block][...])
            table[:, columns_of(d)] = total

    by_home(body)
    sums = lag_sums(table[...])
    for i in range(8):
        out[i : i + 1, :] = sums[:, i * 128 : (i + 1) * 128]


def correlate(moving, onto_far, *fixed):
    vmem = pl.BlockSpec(memory_space=pltpu.VMEM)
    params = pltpu.CompilerParams(vmem_limit_bytes=40 * MIB)
    table = pl.pallas_call(
        main_kernel,
        in_specs=[vmem] * (len(moving) + len(fixed)),
        out_specs=vmem,
        out_shape=jax.ShapeDtypeStruct((BLK, 5 * BLK), jnp.float32),
        compiler_params=params,
        cost_estimate=pl.CostEstimate(
            flops=MAIN_COST, bytes_accessed=4 * MIB, transcendentals=0
        ),
        name="main",
    )(*moving, *fixed)
    return pl.pallas_call(
        tail_kernel,
        in_specs=[vmem] * (2 + len(fixed)),
        out_specs=vmem,
        out_shape=jax.ShapeDtypeStruct((8, 128), jnp.float32),
        scratch_shapes=[pltpu.VMEM((BLK, 5 * BLK), jnp.float32)],
        compiler_params=params,
        name="tail",
    )(table, onto_far, *fixed)


def swap(value, quads, far, flip):
    pairs = [
        ((q * 2 + y) * 2 + c, (q * 2 + (y ^ far)) * 2 + (c ^ flip))
        for q in range(quads) for y in range(2) for c in range(2)
    ]
    return lax.ppermute(value, "ctx", pairs)


def onward(value, quads, flip=0):
    pairs = []
    for q in range(quads):
        for e in range(4):
            core = e % 2 ^ flip
            to = q + 1 - 2 * core
            if 0 <= to < quads:
                pairs.append((q * 4 + e, to * 4 + (e ^ flip)))
    return lax.ppermute(value, "ctx", pairs)


def on_device(queries, keys, values, grad_out):
    quads = lax.axis_size("ctx") // 4
    arrays = (queries, keys, values, grad_out)
    one, two = (BLK, CH), (2, BLK, CH)
    far_moving, give, own_moving = deal(deal_first, "deal_first", [two, one, one], arrays)
    flip_moving = swap(give, quads, 0, 1)
    far_moving = swap(far_moving, quads, 1, 0)
    near_moving = jnp.stack([own_moving, flip_moving])
    beyond = onward(near_moving, quads)
    top, low, give_own, keep, own_fixed = deal(
        deal_second, "deal_second", [(BLK // 2, CH)] * 2 + [one] * 3, arrays
    )
    got = jnp.concatenate([swap(top, quads, 0, 1), swap(low, quads, 0, 1)])
    far_fixed = swap(jnp.stack([keep, got]), quads, 1, 0)
    flip_fixed = swap(give_own, quads, 0, 1)
    last = swap(far_moving[1], quads, 0, 1)
    onto_near = onward(far_moving[0], quads)
    onto_far = onward(far_moving[1], quads, 1)
    moving = (beyond, near_moving, far_moving, last, onto_near)
    part = correlate(moving, onto_far, own_fixed, flip_fixed, far_fixed)
    part = part + swap(part, quads, 0, 1)
    groups = [[q * 4 + y * 2 + c for q in range(quads) for y in range(2)] for c in range(2)]
    spread = jnp.broadcast_to(part[None], (2 * quads, 8, 128))
    gathered = lax.all_to_all(spread, "ctx", 0, 0, axis_index_groups=groups)
    return jnp.sum(gathered.reshape(quads, 2, 8, 128), axis=0).reshape(2, LAGS)


def solution(mesh):
    spec = P("ctx", "ch")
    return jax.shard_map(
        on_device, mesh=mesh, in_specs=(spec,) * 4, out_specs=P("ch", None), check_vma=False
    )
```

```python
import functools

import jax
import jax.numpy as jnp
from jax import lax
from jax.experimental import pallas as pl
from jax.experimental.pallas import tpu as pltpu
from jax.sharding import PartitionSpec as P

BLK = 256
CH = 512
LAGS = 1024
MIB = 1024 * 1024
DEAL_MIB = 56
MAIN_COST = 0
NT = (((1,), (1,)), ((), ()))
BF16 = jnp.bfloat16


def columns(yh, core):
    return pl.ds(pl.multiple_of(yh * 2 * CH + core * CH, CH), CH)


def product(a, b):
    return (a.astype(jnp.float32) * b.astype(jnp.float32)).astype(BF16)


def fetch(core, slots, sems, arrays, wanted):
    queries, keys, values, grad_out = arrays
    mixed, weighted = (keys, values), (queries, grad_out)

    def start(here):
        for i, (same, moving, cols) in enumerate(wanted):
            target = here if same else 1 - here
            pair = mixed if (target == 0) == moving else weighted
            for j in range(2):
                pltpu.make_async_copy(
                    pair[j].at[:, cols], slots.at[2 * i + j], sems.at[2 * i + j]
                ).start()

    pl.when(core == 0)(lambda: start(0))
    pl.when(core == 1)(lambda: start(1))

    def get(i):
        for j in range(2):
            pltpu.make_async_copy(
                keys.at[:, wanted[i][2]], slots.at[2 * i + j], sems.at[2 * i + j]
            ).wait()
        return product(slots[2 * i], slots[2 * i + 1])

    return get


def position():
    place = lax.axis_index("ctx")
    return (place // 2) % 2, place % 2


def deal_first(q, k, v, g, far, slots, sems):
    yh, core = position()
    wanted = (
        (True, True, columns(1 - yh, core)),
        (False, True, columns(1 - yh, 1 - core)),
    )
    get = fetch(core, slots, sems, (q, k, v, g), wanted)
    far[0] = get(0)
    far[1] = get(1)


def deal_moving(q, k, v, g, give, own, slots, sems):
    yh, core = position()
    wanted = (
        (False, True, columns(yh, 1 - core)),
        (True, True, columns(yh, core)),
    )
    get = fetch(core, slots, sems, (q, k, v, g), wanted)
    give[...] = get(0)
    own[...] = get(1)


def deal_fixed(q, k, v, g, top, low, give_own, keep, stay, slots, sems):
    yh, core = position()
    wanted = (
        (False, False, columns(1 - yh, 1 - core)),
        (False, False, columns(yh, 1 - core)),
        (True, False, columns(1 - yh, core)),
        (True, False, columns(yh, core)),
    )
    get = fetch(core, slots, sems, (q, k, v, g), wanted)
    halves = get(0)
    top[...] = halves[: BLK // 2]
    low[...] = halves[BLK // 2 :]
    give_own[...] = get(1)
    keep[...] = get(2)
    stay[...] = get(3)


def deal(body, name, shapes, arrays):
    vmem = pl.BlockSpec(memory_space=pltpu.VMEM)
    return pl.pallas_call(
        body,
        in_specs=[pl.BlockSpec(memory_space=pl.ANY)] * 4,
        out_specs=[vmem] * len(shapes),
        out_shape=[pltpu.VMEM(shape, BF16) for shape in shapes],
        scratch_shapes=[
            pltpu.VMEM((8, BLK, CH), BF16),
            pltpu.SemaphoreType.DMA((8,)),
        ],
        compiler_params=pltpu.CompilerParams(vmem_limit_bytes=DEAL_MIB * MIB),
        name=name,
    )(*arrays)


def lag_sums(table):
    wide = 5 * BLK - 128
    table = table[:128, :wide] + table[128:, 128:]
    total = table[:8]
    for row in range(8, 128, 8):
        total = total + pltpu.roll(table[row : row + 8], wide - row, 1)
    sums = total[:1]
    for row in range(1, 8):
        sums = sums + pltpu.roll(total[row : row + 1], wide - row, 1)
    return sums


def block_dot(core, moving, fixed):
    pair = (moving, fixed) if core == 0 else (fixed, moving)
    return lax.dot_general(*pair, NT, preferred_element_type=jnp.float32)


def by_home(body):
    place = lax.rem(lax.axis_index("ctx"), 4)
    for home in range(4):
        pl.when(place == home)(functools.partial(body, home))


def columns_of(d):
    return pl.ds(d * BLK, BLK)


def early_products(home, table, stay, near, beyond, far, before=None):
    core = home & 1
    here = {home: near.at[0], home ^ 1: near.at[1], home ^ 2: far.at[0]}
    there = {home: beyond.at[0], home ^ 1: beyond.at[1]}
    for d in range(5):
        total = None if before is None else before[:, columns_of(d)]
        for block, ref in stay.items():
            other = block - d if core == 0 else block + d
            source = here if 0 <= other < 4 else there
            if (other & 3) in source:
                dot = block_dot(core, source[other & 3][...], ref[...])
                total = dot if total is None else total + dot
        if total is None:
            total = jnp.zeros((BLK, BLK), jnp.float32)
        table[:, columns_of(d)] = total


def early_kernel(own, flip, beyond, near, far, table):
    by_home(
        lambda home: early_products(
            home, table, {home: own, home ^ 1: flip}, near, beyond, far
        )
    )


def main_kernel(before, fixed, beyond, near, far, table):
    by_home(
        lambda home: early_products(
            home, table, {home ^ 2: fixed.at[0], home ^ 3: fixed.at[1]},
            near, beyond, far, before,
        )
    )


def tail_kernel(
    table_in, on_far, on_near, top, low, own, flip, fixed, out, last, table
):
    last[: BLK // 2] = top[...]
    last[BLK // 2 :] = low[...]

    def body(home):
        core = home & 1
        stay = {home: own, home ^ 1: flip, home ^ 2: fixed.at[0], home ^ 3: fixed.at[1]}
        for d in range(5):
            total = table_in[:, columns_of(d)]
            for block, ref in stay.items():
                other = block - d if core == 0 else block + d
                inside = 0 <= other < 4
                moving = None
                if other & 3 == home ^ 3:
                    moving = last if inside else on_far
                elif other & 3 == home ^ 2 and not inside:
                    moving = on_near
                if moving is not None:
                    total = total + block_dot(core, moving[...], ref[...])
            table[:, columns_of(d)] = total

    by_home(body)
    sums = lag_sums(table[...])
    for i in range(8):
        out[i : i + 1, :] = sums[:, i * 128 : (i + 1) * 128]


def correlate(moving, late, own, flip, fixed):
    vmem = pl.BlockSpec(memory_space=pltpu.VMEM)
    params = pltpu.CompilerParams(vmem_limit_bytes=40 * MIB)

    def table_call(body, name, *operands):
        return pl.pallas_call(
            body,
            in_specs=[vmem] * len(operands),
            out_specs=vmem,
            out_shape=jax.ShapeDtypeStruct((BLK, 5 * BLK), jnp.float32),
            compiler_params=params,
            cost_estimate=pl.CostEstimate(
                flops=MAIN_COST, bytes_accessed=4 * MIB, transcendentals=0
            ),
            name=name,
        )(*operands)

    table = table_call(early_kernel, "early", own, flip, *moving)
    table = table_call(main_kernel, "main", table, fixed, *moving)
    return pl.pallas_call(
        tail_kernel,
        in_specs=[vmem] * (4 + len(late)),
        out_specs=vmem,
        out_shape=jax.ShapeDtypeStruct((8, 128), jnp.float32),
        scratch_shapes=[
            pltpu.VMEM((BLK, CH), BF16),
            pltpu.VMEM((BLK, 5 * BLK), jnp.float32),
        ],
        compiler_params=params,
        name="tail",
    )(table, *late, own, flip, fixed)


def swap(value, quads, far, flip):
    pairs = [
        ((q * 2 + y) * 2 + c, (q * 2 + (y ^ far)) * 2 + (c ^ flip))
        for q in range(quads) for y in range(2) for c in range(2)
    ]
    return lax.ppermute(value, "ctx", pairs)


def onward(value, quads, flip=0):
    pairs = []
    for q in range(quads):
        for e in range(4):
            core = e % 2 ^ flip
            to = q + 1 - 2 * core
            if 0 <= to < quads:
                pairs.append((q * 4 + e, to * 4 + (e ^ flip)))
    return lax.ppermute(value, "ctx", pairs)


def on_device(queries, keys, values, grad_out):
    quads = lax.axis_size("ctx") // 4
    arrays = (queries, keys, values, grad_out)
    one, two, half = (BLK, CH), (2, BLK, CH), (BLK // 2, CH)
    far_moving = swap(deal(deal_first, "deal_first", [two], arrays)[0], quads, 1, 0)
    give, own_moving = deal(deal_moving, "deal_moving", [one, one], arrays)
    top, low, give_own, keep, own_fixed = deal(
        deal_fixed, "deal_fixed", [half, half, one, one, one], arrays
    )
    near_moving = jnp.stack([own_moving, swap(give, quads, 0, 1)])
    beyond = onward(near_moving, quads)
    got = jnp.concatenate([swap(top, quads, 0, 1), swap(low, quads, 0, 1)])
    far_fixed = swap(jnp.stack([keep, got]), quads, 1, 0)
    flip_fixed = swap(give_own, quads, 0, 1)
    last = [swap(far_moving[1, i : i + BLK // 2], quads, 0, 1) for i in (0, BLK // 2)]
    on_near = onward(far_moving[0], quads)
    on_far = onward(far_moving[1], quads, 1)
    moving, late = (beyond, near_moving, far_moving), (on_far, on_near, *last)
    part = correlate(moving, late, own_fixed, flip_fixed, far_fixed)
    part = part + swap(part, quads, 0, 1)
    groups = [[q * 4 + y * 2 + c for q in range(quads) for y in range(2)] for c in range(2)]
    spread = jnp.broadcast_to(part[None], (2 * quads, 8, 128))
    gathered = lax.all_to_all(spread, "ctx", 0, 0, axis_index_groups=groups)
    return jnp.sum(gathered.reshape(quads, 2, 8, 128), axis=0).reshape(2, LAGS)


def solution(mesh):
    spec = P("ctx", "ch")
    return jax.shard_map(
        on_device, mesh=mesh, in_specs=(spec,) * 4, out_specs=P("ch", None), check_vma=False
    )
```

```python
import functools

import jax
import jax.numpy as jnp
from jax import lax
from jax.experimental import pallas as pl
from jax.experimental.pallas import tpu as pltpu
from jax.sharding import PartitionSpec as P

BLK = 256
CH = 512
LAGS = 1024
MIB = 1024 * 1024
DEAL_MIB = 56
MAIN_COST = 0
NT = (((1,), (1,)), ((), ()))
BF16 = jnp.bfloat16


def columns(yh, core):
    return pl.ds(pl.multiple_of(yh * 2 * CH + core * CH, CH), CH)


def product(a, b):
    return (a.astype(jnp.float32) * b.astype(jnp.float32)).astype(BF16)


def fetch(core, slots, sems, arrays, wanted):
    queries, keys, values, grad_out = arrays
    mixed, weighted = (keys, values), (queries, grad_out)

    def start(here):
        for i, (same, moving, cols) in enumerate(wanted):
            target = here if same else 1 - here
            pair = mixed if (target == 1) == moving else weighted
            for j in range(2):
                pltpu.make_async_copy(
                    pair[j].at[:, cols], slots.at[2 * i + j], sems.at[2 * i + j]
                ).start()

    pl.when(core == 0)(lambda: start(0))
    pl.when(core == 1)(lambda: start(1))

    def get(i):
        for j in range(2):
            pltpu.make_async_copy(
                keys.at[:, wanted[i][2]], slots.at[2 * i + j], sems.at[2 * i + j]
            ).wait()
        return product(slots[2 * i], slots[2 * i + 1])

    return get


def position():
    place = lax.axis_index("ctx")
    return (place // 2) % 2, place % 2


def deal_first(q, k, v, g, far, slots, sems):
    yh, core = position()
    wanted = (
        (True, True, columns(1 - yh, core)),
        (False, True, columns(1 - yh, 1 - core)),
    )
    get = fetch(core, slots, sems, (q, k, v, g), wanted)
    far[0] = get(0)
    far[1] = get(1)


def deal_moving(q, k, v, g, give, own, slots, sems):
    yh, core = position()
    wanted = (
        (False, True, columns(yh, 1 - core)),
        (True, True, columns(yh, core)),
    )
    get = fetch(core, slots, sems, (q, k, v, g), wanted)
    give[...] = get(0)
    own[...] = get(1)


def deal_fixed(q, k, v, g, top, low, give_own, keep, stay, slots, sems):
    yh, core = position()
    wanted = (
        (False, False, columns(1 - yh, 1 - core)),
        (False, False, columns(yh, 1 - core)),
        (True, False, columns(1 - yh, core)),
        (True, False, columns(yh, core)),
    )
    get = fetch(core, slots, sems, (q, k, v, g), wanted)
    halves = get(0)
    top[...] = halves[: BLK // 2]
    low[...] = halves[BLK // 2 :]
    give_own[...] = get(1)
    keep[...] = get(2)
    stay[...] = get(3)


def deal(body, name, shapes, arrays):
    vmem = pl.BlockSpec(memory_space=pltpu.VMEM)
    return pl.pallas_call(
        body,
        in_specs=[pl.BlockSpec(memory_space=pl.ANY)] * 4,
        out_specs=[vmem] * len(shapes),
        out_shape=[pltpu.VMEM(shape, BF16) for shape in shapes],
        scratch_shapes=[
            pltpu.VMEM((8, BLK, CH), BF16),
            pltpu.SemaphoreType.DMA((8,)),
        ],
        compiler_params=pltpu.CompilerParams(vmem_limit_bytes=DEAL_MIB * MIB),
        name=name,
    )(*arrays)


def lag_sums(table):
    wide = 5 * BLK - 128
    table = table[:128, :wide] + table[128:, 128:]
    total = table[:8]
    for row in range(8, 128, 8):
        total = total + pltpu.roll(table[row : row + 8], wide - row, 1)
    sums = total[:1]
    for row in range(1, 8):
        sums = sums + pltpu.roll(total[row : row + 1], wide - row, 1)
    return sums


def block_dot(back, moving, fixed):
    pair = (fixed, moving) if back else (moving, fixed)
    return lax.dot_general(*pair, NT, preferred_element_type=jnp.float32)


def by_home(body):
    place = lax.rem(lax.axis_index("ctx"), 4)
    for home in range(4):
        pl.when(place == home)(functools.partial(body, home))


def columns_of(d):
    return pl.ds(d * BLK, BLK)


def early_products(home, table, stay, near, beyond, far, before=None):
    back = home & 1 == 0
    here = {home: near.at[0], home ^ 1: near.at[1], home ^ 2: far.at[0]}
    there = {home: beyond.at[0], home ^ 1: beyond.at[1]}
    for d in range(5):
        total = None if before is None else before[:, columns_of(d)]
        for block, ref in stay.items():
            other = block + d if back else block - d
            source = here if 0 <= other < 4 else there
            if (other & 3) in source:
                dot = block_dot(back, source[other & 3][...], ref[...])
                total = dot if total is None else total + dot
        if total is None:
            total = jnp.zeros((BLK, BLK), jnp.float32)
        table[:, columns_of(d)] = total


def early_kernel(own, flip, beyond, near, far, table):
    by_home(
        lambda home: early_products(
            home, table, {home: own, home ^ 1: flip}, near, beyond, far
        )
    )


def main_kernel(before, fixed, beyond, near, far, table):
    by_home(
        lambda home: early_products(
            home, table, {home ^ 2: fixed.at[0], home ^ 3: fixed.at[1]},
            near, beyond, far, before,
        )
    )


def tail_kernel(
    table_in, on_far, on_near, top, low, own, flip, fixed, out, last, table
):
    last[: BLK // 2] = top[...]
    last[BLK // 2 :] = low[...]

    def body(home):
        back = home & 1 == 0
        stay = {home: own, home ^ 1: flip, home ^ 2: fixed.at[0], home ^ 3: fixed.at[1]}
        for d in range(5):
            total = table_in[:, columns_of(d)]
            for block, ref in stay.items():
                other = block + d if back else block - d
                inside = 0 <= other < 4
                moving = None
                if other & 3 == home ^ 3:
                    moving = last if inside else on_far
                elif other & 3 == home ^ 2 and not inside:
                    moving = on_near
                if moving is not None:
                    total = total + block_dot(back, moving[...], ref[...])
            table[:, columns_of(d)] = total

    by_home(body)
    sums = lag_sums(table[...])
    for i in range(8):
        out[i : i + 1, :] = sums[:, i * 128 : (i + 1) * 128]


def correlate(moving, late, own, flip, fixed):
    vmem = pl.BlockSpec(memory_space=pltpu.VMEM)
    params = pltpu.CompilerParams(vmem_limit_bytes=40 * MIB)

    def table_call(body, name, *operands):
        return pl.pallas_call(
            body,
            in_specs=[vmem] * len(operands),
            out_specs=vmem,
            out_shape=jax.ShapeDtypeStruct((BLK, 5 * BLK), jnp.float32),
            compiler_params=params,
            cost_estimate=pl.CostEstimate(
                flops=MAIN_COST, bytes_accessed=4 * MIB, transcendentals=0
            ),
            name=name,
        )(*operands)

    table = table_call(early_kernel, "early", own, flip, *moving)
    table = table_call(main_kernel, "main", table, fixed, *moving)
    return pl.pallas_call(
        tail_kernel,
        in_specs=[vmem] * (4 + len(late)),
        out_specs=vmem,
        out_shape=jax.ShapeDtypeStruct((8, 128), jnp.float32),
        scratch_shapes=[
            pltpu.VMEM((BLK, CH), BF16),
            pltpu.VMEM((BLK, 5 * BLK), jnp.float32),
        ],
        compiler_params=params,
        name="tail",
    )(table, *late, own, flip, fixed)


def swap(value, quads, far, flip):
    pairs = [
        ((q * 2 + y) * 2 + c, (q * 2 + (y ^ far)) * 2 + (c ^ flip))
        for q in range(quads) for y in range(2) for c in range(2)
    ]
    return lax.ppermute(value, "ctx", pairs)


def onward(value, quads, flip=0):
    pairs = []
    for q in range(quads):
        for e in range(4):
            core = e % 2 ^ flip
            to = q - 1 + 2 * core
            if 0 <= to < quads:
                pairs.append((q * 4 + e, to * 4 + (e ^ flip)))
    return lax.ppermute(value, "ctx", pairs)


def on_device(queries, keys, values, grad_out):
    quads = lax.axis_size("ctx") // 4
    arrays = (queries, keys, values, grad_out)
    one, two, half = (BLK, CH), (2, BLK, CH), (BLK // 2, CH)
    far_moving = swap(deal(deal_first, "deal_first", [two], arrays)[0], quads, 1, 0)
    give, own_moving = deal(deal_moving, "deal_moving", [one, one], arrays)
    top, low, give_own, keep, own_fixed = deal(
        deal_fixed, "deal_fixed", [half, half, one, one, one], arrays
    )
    near_moving = jnp.stack([own_moving, swap(give, quads, 0, 1)])
    beyond = onward(near_moving, quads)
    got = jnp.concatenate([swap(top, quads, 0, 1), swap(low, quads, 0, 1)])
    far_fixed = swap(jnp.stack([keep, got]), quads, 1, 0)
    flip_fixed = swap(give_own, quads, 0, 1)
    last = [swap(far_moving[1, i : i + BLK // 2], quads, 0, 1) for i in (0, BLK // 2)]
    on_near = onward(far_moving[0], quads)
    on_far = onward(far_moving[1], quads, 1)
    moving, late = (beyond, near_moving, far_moving), (on_far, on_near, *last)
    part = correlate(moving, late, own_fixed, flip_fixed, far_fixed)
    part = part + swap(part, quads, 0, 1)
    groups = [[q * 4 + y * 2 + c for q in range(quads) for y in range(2)] for c in range(2)]
    spread = jnp.broadcast_to(part[None], (2 * quads, 8, 128))
    gathered = lax.all_to_all(spread, "ctx", 0, 0, axis_index_groups=groups)
    return jnp.sum(gathered.reshape(quads, 2, 8, 128), axis=0).reshape(2, LAGS)


def solution(mesh):
    spec = P("ctx", "ch")
    return jax.shard_map(
        on_device, mesh=mesh, in_specs=(spec,) * 4, out_specs=P("ch", None), check_vma=False
    )
```

```python
import functools

import jax
import jax.numpy as jnp
from jax import lax
from jax.experimental import pallas as pl
from jax.experimental.pallas import tpu as pltpu
from jax.sharding import PartitionSpec as P

BLK = 256
CH = 512
LAGS = 1024
MIB = 1024 * 1024
DEAL_MIB = 56
MAIN_COST = 0
NT = (((1,), (1,)), ((), ()))
BF16 = jnp.bfloat16


def columns(yh, core):
    return pl.ds(pl.multiple_of(yh * 2 * CH + core * CH, CH), CH)


def product(a, b):
    return (a.astype(jnp.float32) * b.astype(jnp.float32)).astype(BF16)


def fetch(core, slots, sems, arrays, wanted):
    queries, keys, values, grad_out = arrays
    mixed, weighted = (keys, values), (queries, grad_out)

    def start(here):
        for i, (same, moving, cols) in enumerate(wanted):
            target = here if same else 1 - here
            pair = mixed if (target == 1) == moving else weighted
            for j in range(2):
                pltpu.make_async_copy(
                    pair[j].at[:, cols], slots.at[2 * i + j], sems.at[2 * i + j]
                ).start()

    pl.when(core == 0)(lambda: start(0))
    pl.when(core == 1)(lambda: start(1))

    def get(i):
        for j in range(2):
            pltpu.make_async_copy(
                keys.at[:, wanted[i][2]], slots.at[2 * i + j], sems.at[2 * i + j]
            ).wait()
        return product(slots[2 * i], slots[2 * i + 1])

    return get


def position():
    place = lax.axis_index("ctx")
    return (place // 2) % 2, place % 2


def deal_first(q, k, v, g, far, slots, sems):
    yh, core = position()
    wanted = (
        (True, True, columns(1 - yh, core)),
        (False, True, columns(1 - yh, 1 - core)),
    )
    get = fetch(core, slots, sems, (q, k, v, g), wanted)
    far[0] = get(0)
    far[1] = get(1)


def deal_moving(q, k, v, g, give, own, slots, sems):
    yh, core = position()
    wanted = (
        (False, True, columns(yh, 1 - core)),
        (True, True, columns(yh, core)),
    )
    get = fetch(core, slots, sems, (q, k, v, g), wanted)
    give[...] = get(0)
    own[...] = get(1)


def deal_fixed(q, k, v, g, top, low, give_own, keep, stay, slots, sems):
    yh, core = position()
    wanted = (
        (False, False, columns(1 - yh, 1 - core)),
        (False, False, columns(yh, 1 - core)),
        (True, False, columns(1 - yh, core)),
        (True, False, columns(yh, core)),
    )
    get = fetch(core, slots, sems, (q, k, v, g), wanted)
    halves = get(0)
    top[...] = halves[: BLK // 2]
    low[...] = halves[BLK // 2 :]
    give_own[...] = get(1)
    keep[...] = get(2)
    stay[...] = get(3)


def deal(body, name, shapes, arrays):
    vmem = pl.BlockSpec(memory_space=pltpu.VMEM)
    return pl.pallas_call(
        body,
        in_specs=[pl.BlockSpec(memory_space=pl.ANY)] * 4,
        out_specs=[vmem] * len(shapes),
        out_shape=[pltpu.VMEM(shape, BF16) for shape in shapes],
        scratch_shapes=[
            pltpu.VMEM((8, BLK, CH), BF16),
            pltpu.SemaphoreType.DMA((8,)),
        ],
        compiler_params=pltpu.CompilerParams(vmem_limit_bytes=DEAL_MIB * MIB),
        name=name,
    )(*arrays)


def lag_sums(table):
    wide = 5 * BLK - 128
    table = table[:128, :wide] + table[128:, 128:]
    total = table[:8]
    for row in range(8, 128, 8):
        total = total + pltpu.roll(table[row : row + 8], wide - row, 1)
    sums = total[:1]
    for row in range(1, 8):
        sums = sums + pltpu.roll(total[row : row + 1], wide - row, 1)
    return sums


def block_dot(back, moving, fixed):
    pair = (fixed, moving) if back else (moving, fixed)
    return lax.dot_general(*pair, NT, preferred_element_type=jnp.float32)


def by_home(body):
    place = lax.rem(lax.axis_index("ctx"), 4)
    for home in range(4):
        pl.when(place == home)(functools.partial(body, home))


def columns_of(d):
    return pl.ds(d * BLK, BLK)


def early_products(home, table, stay, near, beyond, far, before=None, last=None, others=()):
    back = home & 1 == 0
    here = {home: near.at[0], home ^ 1: near.at[1], home ^ 2: far.at[0]}
    there = {home: beyond.at[0], home ^ 1: beyond.at[1]}
    for d in range(5):
        total = None if before is None else before[:, columns_of(d)]
        for block, ref in stay.items():
            other = block + d if back else block - d
            source = here if 0 <= other < 4 else there
            if (other & 3) in source:
                dot = block_dot(back, source[other & 3][...], ref[...])
                total = dot if total is None else total + dot
            elif last is not None and 0 <= other < 4:
                total = total + block_dot(back, last[...], ref[...])
        for block, ref in others:
            other = block + d if back else block - d
            if other == home ^ 3:
                total = total + block_dot(back, last[...], ref[...])
        if total is None:
            total = jnp.zeros((BLK, BLK), jnp.float32)
        table[:, columns_of(d)] = total


def early_kernel(own, flip, beyond, near, far, table):
    by_home(
        lambda home: early_products(
            home, table, {home: own, home ^ 1: flip}, near, beyond, far
        )
    )


def main_kernel(before, top, low, own, flip, fixed, beyond, near, far, table, last):
    last[: BLK // 2] = top[...]
    last[BLK // 2 :] = low[...]
    by_home(
        lambda home: early_products(
            home, table, {home ^ 2: fixed.at[0], home ^ 3: fixed.at[1]},
            near, beyond, far, before, last, ((home, own), (home ^ 1, flip)),
        )
    )


def tail_kernel(
    table_in, on_near, on_far, own, flip, fixed, out, table
):
    def body(home):
        back = home & 1 == 0
        stay = {home: own, home ^ 1: flip, home ^ 2: fixed.at[0], home ^ 3: fixed.at[1]}
        for d in range(5):
            total = table_in[:, columns_of(d)]
            for block, ref in stay.items():
                other = block + d if back else block - d
                inside = 0 <= other < 4
                moving = None
                if other & 3 == home ^ 3 and not inside:
                    moving = on_far
                elif other & 3 == home ^ 2 and not inside:
                    moving = on_near
                if moving is not None:
                    total = total + block_dot(back, moving[...], ref[...])
            table[:, columns_of(d)] = total

    by_home(body)
    sums = lag_sums(table[...])
    for i in range(8):
        out[i : i + 1, :] = sums[:, i * 128 : (i + 1) * 128]


def correlate(moving, last, late, own, flip, fixed):
    vmem = pl.BlockSpec(memory_space=pltpu.VMEM)
    params = pltpu.CompilerParams(vmem_limit_bytes=40 * MIB)

    def table_call(body, name, scratch, *operands):
        return pl.pallas_call(
            body,
            in_specs=[vmem] * len(operands),
            out_specs=vmem,
            out_shape=jax.ShapeDtypeStruct((BLK, 5 * BLK), jnp.float32),
            scratch_shapes=scratch,
            compiler_params=params,
            cost_estimate=pl.CostEstimate(
                flops=MAIN_COST, bytes_accessed=4 * MIB, transcendentals=0
            ),
            name=name,
        )(*operands)

    table = table_call(early_kernel, "early", [], own, flip, *moving)
    table = table_call(
        main_kernel, "main", [pltpu.VMEM((BLK, CH), BF16)],
        table, *last, own, flip, fixed, *moving,
    )
    return pl.pallas_call(
        tail_kernel,
        in_specs=[vmem] * (4 + len(late)),
        out_specs=vmem,
        out_shape=jax.ShapeDtypeStruct((8, 128), jnp.float32),
        scratch_shapes=[pltpu.VMEM((BLK, 5 * BLK), jnp.float32)],
        compiler_params=params,
        name="tail",
    )(table, *late, own, flip, fixed)


def swap(value, quads, far, flip):
    pairs = [
        ((q * 2 + y) * 2 + c, (q * 2 + (y ^ far)) * 2 + (c ^ flip))
        for q in range(quads) for y in range(2) for c in range(2)
    ]
    return lax.ppermute(value, "ctx", pairs)


def onward(value, quads, flip=0):
    pairs = []
    for q in range(quads):
        for e in range(4):
            core = e % 2 ^ flip
            to = q - 1 + 2 * core
            if 0 <= to < quads:
                pairs.append((q * 4 + e, to * 4 + (e ^ flip)))
    return lax.ppermute(value, "ctx", pairs)


def on_device(queries, keys, values, grad_out):
    quads = lax.axis_size("ctx") // 4
    arrays = (queries, keys, values, grad_out)
    one, two, half = (BLK, CH), (2, BLK, CH), (BLK // 2, CH)
    far_moving = swap(deal(deal_first, "deal_first", [two], arrays)[0], quads, 1, 0)
    give, own_moving = deal(deal_moving, "deal_moving", [one, one], arrays)
    top, low, give_own, keep, own_fixed = deal(
        deal_fixed, "deal_fixed", [half, half, one, one, one], arrays
    )
    near_moving = jnp.stack([own_moving, swap(give, quads, 0, 1)])
    beyond = onward(near_moving, quads)
    got = jnp.concatenate([swap(top, quads, 0, 1), swap(low, quads, 0, 1)])
    far_fixed = swap(jnp.stack([keep, got]), quads, 1, 0)
    flip_fixed = swap(give_own, quads, 0, 1)
    last = [swap(far_moving[1, i : i + BLK // 2], quads, 0, 1) for i in (0, BLK // 2)]
    on_near = onward(far_moving[0], quads)
    on_far = onward(far_moving[1], quads, 1)
    moving, late = (beyond, near_moving, far_moving), (on_near, on_far)
    part = correlate(moving, last, late, own_fixed, flip_fixed, far_fixed)
    part = part + swap(part, quads, 0, 1)
    groups = [[q * 4 + y * 2 + c for q in range(quads) for y in range(2)] for c in range(2)]
    spread = jnp.broadcast_to(part[None], (2 * quads, 8, 128))
    gathered = lax.all_to_all(spread, "ctx", 0, 0, axis_index_groups=groups)
    return jnp.sum(gathered.reshape(quads, 2, 8, 128), axis=0).reshape(2, LAGS)


def solution(mesh):
    spec = P("ctx", "ch")
    return jax.shard_map(
        on_device, mesh=mesh, in_specs=(spec,) * 4, out_specs=P("ch", None), check_vma=False
    )
```

```python
import functools

import jax
import jax.numpy as jnp
from jax import lax
from jax.experimental import pallas as pl
from jax.experimental.pallas import tpu as pltpu
from jax.sharding import PartitionSpec as P

BLK = 256
CH = 512
LAGS = 1024
MIB = 1024 * 1024
DEAL_MIB = 56
MAIN_COST = 0
NT = (((1,), (1,)), ((), ()))
BF16 = jnp.bfloat16


def columns(yh, core):
    return pl.ds(pl.multiple_of(yh * 2 * CH + core * CH, CH), CH)


def product(a, b):
    return (a.astype(jnp.float32) * b.astype(jnp.float32)).astype(BF16)


def fetch(core, slots, sems, arrays, wanted):
    queries, keys, values, grad_out = arrays
    mixed, weighted = (keys, values), (queries, grad_out)

    def start(here):
        for i, (same, moving, cols) in enumerate(wanted):
            target = here if same else 1 - here
            pair = mixed if (target == 1) == moving else weighted
            for j in range(2):
                pltpu.make_async_copy(
                    pair[j].at[:, cols], slots.at[2 * i + j], sems.at[2 * i + j]
                ).start()

    pl.when(core == 0)(lambda: start(0))
    pl.when(core == 1)(lambda: start(1))

    def get(i):
        for j in range(2):
            pltpu.make_async_copy(
                keys.at[:, wanted[i][2]], slots.at[2 * i + j], sems.at[2 * i + j]
            ).wait()
        return product(slots[2 * i], slots[2 * i + 1])

    return get


def position():
    place = lax.axis_index("ctx")
    return (place // 2) % 2, place % 2


def deal_first(q, k, v, g, far, slots, sems):
    yh, core = position()
    wanted = (
        (True, True, columns(1 - yh, core)),
        (False, True, columns(1 - yh, 1 - core)),
    )
    get = fetch(core, slots, sems, (q, k, v, g), wanted)
    far[0] = get(0)
    far[1] = get(1)


def deal_moving(q, k, v, g, give, own, slots, sems):
    yh, core = position()
    wanted = (
        (False, True, columns(yh, 1 - core)),
        (True, True, columns(yh, core)),
    )
    get = fetch(core, slots, sems, (q, k, v, g), wanted)
    give[...] = get(0)
    own[...] = get(1)


def deal_fixed(q, k, v, g, top, low, give_own, keep, stay, slots, sems):
    yh, core = position()
    wanted = (
        (False, False, columns(1 - yh, 1 - core)),
        (False, False, columns(yh, 1 - core)),
        (True, False, columns(1 - yh, core)),
        (True, False, columns(yh, core)),
    )
    get = fetch(core, slots, sems, (q, k, v, g), wanted)
    halves = get(0)
    top[...] = halves[: BLK // 2]
    low[...] = halves[BLK // 2 :]
    give_own[...] = get(1)
    keep[...] = get(2)
    stay[...] = get(3)


def deal(body, name, shapes, arrays):
    vmem = pl.BlockSpec(memory_space=pltpu.VMEM)
    return pl.pallas_call(
        body,
        in_specs=[pl.BlockSpec(memory_space=pl.ANY)] * 4,
        out_specs=[vmem] * len(shapes),
        out_shape=[pltpu.VMEM(shape, BF16) for shape in shapes],
        scratch_shapes=[
            pltpu.VMEM((8, BLK, CH), BF16),
            pltpu.SemaphoreType.DMA((8,)),
        ],
        compiler_params=pltpu.CompilerParams(vmem_limit_bytes=DEAL_MIB * MIB),
        name=name,
    )(*arrays)


def lag_sums(table):
    wide = 5 * BLK - 128
    table = table[:128, :wide] + table[128:, 128:]
    total = table[:8]
    for row in range(8, 128, 8):
        total = total + pltpu.roll(table[row : row + 8], wide - row, 1)
    sums = total[:1]
    for row in range(1, 8):
        sums = sums + pltpu.roll(total[row : row + 1], wide - row, 1)
    return sums


def block_dot(back, moving, fixed):
    pair = (fixed, moving) if back else (moving, fixed)
    return lax.dot_general(*pair, NT, preferred_element_type=jnp.float32)


def by_home(body):
    place = lax.rem(lax.axis_index("ctx"), 4)
    for home in range(4):
        pl.when(place == home)(functools.partial(body, home))


def columns_of(d):
    return pl.ds(d * BLK, BLK)


def early_products(home, table, stay, near, beyond, far, before=None, last=None, others=()):
    back = home & 1 == 0
    here = {home: near.at[0], home ^ 1: near.at[1], home ^ 2: far.at[0]}
    there = {home: beyond.at[0], home ^ 1: beyond.at[1]}
    for d in range(5):
        total = None if before is None else before[:, columns_of(d)]
        for block, ref in stay.items():
            other = block + d if back else block - d
            source = here if 0 <= other < 4 else there
            if (other & 3) in source:
                dot = block_dot(back, source[other & 3][...], ref[...])
                total = dot if total is None else total + dot
            elif last is not None and 0 <= other < 4:
                total = total + block_dot(back, last[...], ref[...])
        for block, ref in others:
            other = block + d if back else block - d
            if other == home ^ 3:
                total = total + block_dot(back, last[...], ref[...])
        if total is None:
            total = jnp.zeros((BLK, BLK), jnp.float32)
        table[:, columns_of(d)] = total


def early_kernel(own, flip, beyond, near, far, table):
    by_home(
        lambda home: early_products(
            home, table, {home: own, home ^ 1: flip}, near, beyond, far
        )
    )


def main_kernel(before, top, low, own, flip, fixed, beyond, near, far, table, last):
    last[: BLK // 2] = top[...]
    last[BLK // 2 :] = low[...]
    by_home(
        lambda home: early_products(
            home, table, {home ^ 2: fixed.at[0], home ^ 3: fixed.at[1]},
            near, beyond, far, before, last, ((home, own), (home ^ 1, flip)),
        )
    )


def tail_kernel(
    table_in, on_near, on_far, own, flip, fixed, out, table
):
    def body(home):
        back = home & 1 == 0
        stay = {home: own, home ^ 1: flip, home ^ 2: fixed.at[0], home ^ 3: fixed.at[1]}
        for d in range(5):
            total = table_in[:, columns_of(d)]
            for block, ref in stay.items():
                other = block + d if back else block - d
                inside = 0 <= other < 4
                moving = None
                if other & 3 == home ^ 3 and not inside:
                    moving = on_far
                elif other & 3 == home ^ 2 and not inside:
                    moving = on_near
                if moving is not None:
                    total = total + block_dot(back, moving[...], ref[...])
            table[:, columns_of(d)] = total

    by_home(body)
    sums = lag_sums(table[...])
    for i in range(8):
        out[i : i + 1, :] = sums[:, i * 128 : (i + 1) * 128]


def correlate(moving, last, late, own, flip, fixed):
    vmem = pl.BlockSpec(memory_space=pltpu.VMEM)
    params = pltpu.CompilerParams(vmem_limit_bytes=40 * MIB)

    def table_call(body, name, scratch, *operands):
        return pl.pallas_call(
            body,
            in_specs=[vmem] * len(operands),
            out_specs=vmem,
            out_shape=jax.ShapeDtypeStruct((BLK, 5 * BLK), jnp.float32),
            scratch_shapes=scratch,
            compiler_params=params,
            cost_estimate=pl.CostEstimate(
                flops=MAIN_COST, bytes_accessed=4 * MIB, transcendentals=0
            ),
            name=name,
        )(*operands)

    table = table_call(early_kernel, "early", [], own, flip, *moving)
    table = table_call(
        main_kernel, "main", [pltpu.VMEM((BLK, CH), BF16)],
        table, *last, own, flip, fixed, *moving,
    )
    return pl.pallas_call(
        tail_kernel,
        in_specs=[vmem] * (4 + len(late)),
        out_specs=vmem,
        out_shape=jax.ShapeDtypeStruct((8, 128), jnp.float32),
        scratch_shapes=[pltpu.VMEM((BLK, 5 * BLK), jnp.float32)],
        compiler_params=params,
        name="tail",
    )(table, *late, own, flip, fixed)


def swap(value, quads, far, flip):
    pairs = [
        ((q * 2 + y) * 2 + c, (q * 2 + (y ^ far)) * 2 + (c ^ flip))
        for q in range(quads) for y in range(2) for c in range(2)
    ]
    return lax.ppermute(value, "ctx", pairs)


def onward(value, quads, flip=0):
    pairs = []
    for q in range(quads):
        for e in range(4):
            core = e % 2 ^ flip
            to = q - 1 + 2 * core
            if 0 <= to < quads:
                pairs.append((q * 4 + e, to * 4 + (e ^ flip)))
    return lax.ppermute(value, "ctx", pairs)


def on_device(queries, keys, values, grad_out):
    quads = lax.axis_size("ctx") // 4
    arrays = (queries, keys, values, grad_out)
    one, two, half = (BLK, CH), (2, BLK, CH), (BLK // 2, CH)
    far_moving = swap(deal(deal_first, "deal_first", [two], arrays)[0], quads, 1, 0)
    give, own_moving = deal(deal_moving, "deal_moving", [one, one], arrays)
    top, low, give_own, keep, own_fixed = deal(
        deal_fixed, "deal_fixed", [half, half, one, one, one], arrays
    )
    near_moving = jnp.stack([own_moving, swap(give, quads, 0, 1)])
    beyond = onward(near_moving, quads)
    got = jnp.concatenate([swap(top, quads, 0, 1), swap(low, quads, 0, 1)])
    far_fixed = swap(jnp.stack([keep, got]), quads, 1, 0)
    flip_fixed = swap(give_own, quads, 0, 1)
    last = [swap(far_moving[1, i : i + BLK // 2], quads, 0, 1) for i in (0, BLK // 2)]
    on_near = onward(far_moving[0], quads)
    on_far = onward(far_moving[1], quads, 1)
    moving, late = (beyond, near_moving, far_moving), (on_near, on_far)
    part = correlate(moving, last, late, own_fixed, flip_fixed, far_fixed)
    groups = [[q * 4 + y * 2 + c for q in range(quads) for y in range(2)] for c in range(2)]
    spread = jnp.broadcast_to(part[None], (2 * quads, 8, 128))
    gathered = lax.all_to_all(spread, "ctx", 0, 0, axis_index_groups=groups)
    sums = jnp.sum(gathered.reshape(quads, 2, 8, 128), axis=0)
    return (sums + swap(sums, quads, 0, 1)).reshape(2, LAGS)


def solution(mesh):
    spec = P("ctx", "ch")
    return jax.shard_map(
        on_device, mesh=mesh, in_specs=(spec,) * 4, out_specs=P("ch", None), check_vma=False
    )
```
